128 devices in a mesh: dp: 2 (over z_hi), pipe: 8 (over z_lo, x), mp: 8 (over y, core).
Axes of the slice: x: 4, y: 4, z: 4 (z_hi: 2, z_lo: 2; z = z_hi * 2 + z_lo), core: 2. Of those that a mesh axis runs over, the one named last changes fastest.
Arguments:
- inputs: bfloat16 [4, 128, 1024], P(None, 'dp', 'mp'), may hold values from -6 to 6
- cotangent: bfloat16 [4, 128, 1024], P(None, 'dp', 'mp'), may hold values from -6 to 6
- gain: float32 [8, 1024], P('pipe'), may hold values from 0.25 to 1.75
- weight_in: bfloat16 [8, 1024, 32768], P('pipe', None, 'mp'), may hold values from -0.1875 to 0.1875
- weight_out: bfloat16 [8, 32768, 1024], P('pipe', 'mp'), may hold values from -0.03125 to 0.03125
Outputs:
- grad_in: bfloat16 [8, 1024, 32768], P('pipe', 'dp', 'mp')
- grad_out: bfloat16 [8, 32768, 1024], P('pipe', 'mp', 'dp')
- grad_gain: float32 [8, 1024], P('pipe', 'mp')
The draws below stay inside these ranges and needn't reach their ends.
All inputs are finite; a program needn't handle non-finite values.
Results may differ from the reference program's by a relative error of at most 0.023.
Values may be sent and summed in bfloat16 or wider, within the bound.
No kernel may reach another device: no remote copies, remote signals or barrier semaphores. Data moves between devices by JAX's collectives and lax.ppermute only.
A program may use at most 128 MiB of HBM per device.

```python
import math
import jax
import jax.numpy as jnp
from jax import lax

D = 1024
FF = 32768
MICRO = 4
SEGMENTS = 8
MB_TOK = 128


def shard_levels(rng, shape, split, low, largest):
    def one(dim, shards_of):
        steps = jax.random.uniform(jax.random.fold_in(jax.random.fold_in(rng, 6), dim), (shards_of,), jnp.float32, low / len(split), largest / len(split))
        return jnp.repeat(jnp.exp(steps), shape[dim] // shards_of).reshape((-1,) + (1,) * (len(shape) - dim - 1))

    level = one(*split[0])
    for cut in split[1:]:
        level = level * one(*cut)
    return level


def gaussian(stream_key, extent, scale, most, pieces=(), kind=jnp.bfloat16):
    entries = jax.random.normal(stream_key, extent, jnp.float32) * scale
    if len(pieces) > 0:
        entries = shard_levels(stream_key, extent, pieces, -0.22, 0.18) * entries
    return jnp.clip(entries, min=-most, max=most).astype(kind)


def setup_inputs(seed: int = 0) -> dict:
    streams_of = jax.random.split(jax.random.key(seed), 6)
    inputs = gaussian(streams_of[0], (MICRO, MB_TOK, D), 1.0, 6.0, ((1, 2), (2, 8)))
    cotangent = gaussian(streams_of[1], (MICRO, MB_TOK, D), 1.0, 6.0, ((1, 2), (2, 8)))
    gain = jnp.clip(1.0 + 0.15 * jax.random.normal(streams_of[2], (SEGMENTS, D), jnp.float32), 0.25, 1.75)
    weight_in = gaussian(streams_of[3], (SEGMENTS, D, FF), D ** -0.5, 0.1875, ((0, 8), (2, 8)))
    weight_out = gaussian(streams_of[4], (SEGMENTS, FF, D), FF ** -0.5, 0.03125, ((0, 8), (1, 8)))
    return dict(inputs=inputs, cotangent=cotangent, gain=gain, weight_in=weight_in, weight_out=weight_out)


GELU_COEF = math.sqrt(2.0 / math.pi)
CUBIC_COEF = 0.044715
NORM_EPS = 1e-06

def gelu_parts(values):
    tangent = jnp.tanh(GELU_COEF * (values + CUBIC_COEF * values * values * values))
    output = 0.5 * values * (1.0 + tangent)
    derivative = 0.5 * (1.0 + tangent) + 0.5 * values * (1.0 - tangent * tangent) * GELU_COEF * (1.0 + 3.0 * CUBIC_COEF * values * values)
    return (output, derivative)

def reference(inputs, cotangent, gain, weight_in, weight_out):
    hidden_rows = inputs.reshape(-1, D)
    saved = []
    for segment in range(SEGMENTS):
        values = hidden_rows.astype(jnp.float32)
        inv_rms = lax.rsqrt(lax.optimization_barrier(jnp.mean(values * values, axis=1, keepdims=True)) + NORM_EPS)
        normed = (values * inv_rms * gain[segment]).astype(jnp.bfloat16)
        gate_input = jnp.dot(normed, weight_in[segment], preferred_element_type=jnp.float32)
        activated = gelu_parts(gate_input)[0].astype(jnp.bfloat16)
        branch = jnp.dot(activated, weight_out[segment], preferred_element_type=jnp.float32)
        saved.append((values, inv_rms, normed))
        hidden_rows = (values + branch).astype(jnp.bfloat16)
    grad_rows = cotangent.reshape(-1, D).astype(jnp.float32)
    grads_in = [None] * SEGMENTS
    grads_out = [None] * SEGMENTS
    grads_gain = [None] * SEGMENTS
    for segment in reversed(range(SEGMENTS)):
        values, inv_rms, normed = saved[segment]
        gate_input = jnp.dot(normed, weight_in[segment], preferred_element_type=jnp.float32)
        output_vals, slopes = gelu_parts(gate_input)
        activated = output_vals.astype(jnp.bfloat16)
        out_grad = grad_rows.astype(jnp.bfloat16)
        inner_grad = jnp.dot(out_grad, weight_out[segment].T, preferred_element_type=jnp.float32)
        pre_grad = (inner_grad * slopes).astype(jnp.bfloat16)
        grads_in[segment] = jnp.dot(normed.T, pre_grad, preferred_element_type=jnp.float32).astype(jnp.bfloat16)
        grads_out[segment] = jnp.dot(activated.T, out_grad, preferred_element_type=jnp.float32).astype(jnp.bfloat16)
        norm_grad = jnp.dot(pre_grad, weight_in[segment].T, preferred_element_type=jnp.float32)
        unit_rows = values * inv_rms
        grads_gain[segment] = lax.optimization_barrier(jnp.sum(norm_grad * unit_rows, axis=0))
        scaled = norm_grad * gain[segment]
        row_dot = lax.optimization_barrier(jnp.sum(scaled * unit_rows, axis=1, keepdims=True))
        grad_rows = grad_rows + inv_rms * (scaled - unit_rows * row_dot / D)
    return (jnp.stack(grads_in), jnp.stack(grads_out), jnp.stack(grads_gain))
```

```python
import functools
import math

import jax
import jax.numpy as jnp
from jax import lax
from jax.experimental import pallas as pl
from jax.experimental.pallas import tpu as pltpu
from jax.sharding import PartitionSpec as P

GELU_COEF = math.sqrt(2.0 / math.pi)
CUBIC_COEF = 0.044715
NORM_EPS = 1e-06
BF16 = jnp.bfloat16
F32 = jnp.float32
NT = (((1,), (1,)), ((), ()))
TN = (((0,), (0,)), ((), ()))
MIB = 2**20
TILE = 512
VMEM = pltpu.VMEM
IN_VMEM = pl.BlockSpec(memory_space=pltpu.VMEM)
IN_SMEM = pl.BlockSpec(memory_space=pltpu.SMEM)
ANYWHERE = pl.BlockSpec(memory_space=pl.ANY)
IN_HBM = pl.BlockSpec(memory_space=pltpu.HBM)


def params(mib):
    return pltpu.CompilerParams(vmem_limit_bytes=int(mib * MIB))


def gelu_both(a):
    a2 = a * a
    t = jnp.tanh(a * (GELU_COEF + (GELU_COEF * CUBIC_COEF) * a2))
    h = 0.5 + 0.5 * t
    z = a * h
    slope = h + (a * (0.5 - 0.5 * t * t)) * (GELU_COEF + (3.0 * GELU_COEF * CUBIC_COEF) * a2)
    return z, slope


def load_body(wi, wo, wi_out, wo_out, sems):
    first = pltpu.make_async_copy(wi, wi_out, sems.at[0])
    second = pltpu.make_async_copy(wo, wo_out, sems.at[1])
    first.start()
    second.start()
    first.wait()
    second.wait()


def load_weights(wi, wo):
    return pl.pallas_call(
        load_body,
        out_shape=(VMEM(wi.shape, wi.dtype), VMEM(wo.shape, wo.dtype)),
        in_specs=[IN_HBM] * 2,
        out_specs=[IN_VMEM] * 2,
        scratch_shapes=[pltpu.SemaphoreType.DMA((2,))],
        compiler_params=params(1),
        name="load_weights",
    )(wi, wo)


def alloc_body(*refs):
    refs[-1][...] = jnp.zeros_like(refs[-1])


def alloc(shapes, dtypes):
    return pl.pallas_call(
        alloc_body,
        out_shape=tuple(VMEM(s, d) for s, d in zip(shapes, dtypes)),
        out_specs=[IN_VMEM] * len(shapes),
        compiler_params=params(1),
        name="alloc",
    )()


def norm_body(t, flags, a0, a1, a2, a3, gain, n_in, r_in, u_out, n_save, r_save):
    rows = a0.shape[0]

    @pl.when(flags[t] > 0)
    def _():
        for d, piece in enumerate((a0, a1, a2, a3)):
            x = piece[...].astype(F32)
            r = lax.rsqrt(jnp.mean(x * x, axis=1, keepdims=True) + NORM_EPS)
            n = x * r
            u_out[d * rows : (d + 1) * rows, :] = (n * gain[...]).astype(BF16)
            if d == 0:
                n_save[...] = n
                r_save[...] = jnp.broadcast_to(r, r_save.shape)


def norm_call(t, flags, pieces, gain, n_save, r_save):
    rows, width = pieces[0].shape
    return pl.pallas_call(
        functools.partial(norm_body, t),
        out_shape=(
            jax.ShapeDtypeStruct((4 * rows, width), BF16),
            VMEM(n_save.shape, F32),
            VMEM(r_save.shape, F32),
        ),
        in_specs=[IN_SMEM] + [IN_VMEM] * 7,
        out_specs=[IN_VMEM] * 3,
        input_output_aliases={6: 1, 7: 2},
        compiler_params=params(4),
        name=f"norm_t{t}",
    )(flags, *pieces, gain, n_save, r_save)


def forward_body(t, last, flags, u_own, u_oth, wi, wo, z_in, s_in, us_in, p_own, p_oth, z, s, us, acc, sems):
    half = u_own.shape[0]
    first = pltpu.make_async_copy(u_own, us.at[pl.ds(0, half)], sems.at[0])
    second = pltpu.make_async_copy(u_oth, us.at[pl.ds(half, half)], sems.at[1])

    @pl.when(flags[t] > 0)
    def _():
        first.start()
        second.start()
        u = jnp.concatenate([u_own[...], u_oth[...]], axis=0)
        for j in range(wi.shape[1] // TILE):
            cols = slice(j * TILE, (j + 1) * TILE)
            a = jnp.dot(u, wi[:, cols], preferred_element_type=F32)
            zf, slope = gelu_both(a)
            zb = zf.astype(BF16)
            z[:, cols] = zb
            s[:, cols] = slope.astype(BF16)
            if not last:
                d = jnp.dot(zb, wo[cols, :], preferred_element_type=F32)
                if j == 0:
                    acc[...] = d
                else:
                    acc[...] += d
        if not last:
            p_own[...] = acc[:half]
            p_oth[...] = acc[half:].astype(BF16)
        first.wait()
        second.wait()


def forward_call(t, last, flags, u_own, u_oth, wi, wo, z, s, us):
    shape = u_own.shape
    return pl.pallas_call(
        functools.partial(forward_body, t, last),
        out_shape=(
            VMEM(shape, F32),
            jax.ShapeDtypeStruct(shape, BF16),
            VMEM(z.shape, BF16),
            VMEM(s.shape, BF16),
            jax.ShapeDtypeStruct(us.shape, BF16),
        ),
        in_specs=[IN_SMEM] + [IN_VMEM] * 6 + [IN_HBM],
        out_specs=[IN_VMEM] * 4 + [IN_HBM],
        scratch_shapes=[VMEM((2 * shape[0], shape[1]), F32), pltpu.SemaphoreType.DMA((2,))],
        input_output_aliases={5: 2, 6: 3, 7: 4},
        compiler_params=params(14),
        name=f"forward_t{t}",
    )(flags, u_own, u_oth, wi, wo, z, s, us)


def backward_body(t, flags, e_own, e_oth, wi, wo, s, p_in, es_in, q_own, q_oth, p, es, acc, sems):
    half = e_own.shape[0]
    first = pltpu.make_async_copy(e_own, es.at[pl.ds(0, half)], sems.at[0])
    second = pltpu.make_async_copy(e_oth, es.at[pl.ds(half, half)], sems.at[1])

    @pl.when(flags[t] > 0)
    def _():
        first.start()
        second.start()
        e = jnp.concatenate([e_own[...], e_oth[...]], axis=0)
        for j in range(wi.shape[1] // TILE):
            cols = slice(j * TILE, (j + 1) * TILE)
            dz = lax.dot_general(e, wo[cols, :], NT, preferred_element_type=F32)
            pb = (dz * s[:, cols].astype(F32)).astype(BF16)
            p[:, cols] = pb
            d = lax.dot_general(pb, wi[:, cols], NT, preferred_element_type=F32)
            if j == 0:
                acc[...] = d
            else:
                acc[...] += d
        q_own[...] = acc[:half]
        q_oth[...] = acc[half:].astype(BF16)
        first.wait()
        second.wait()


def backward_call(t, flags, e_own, e_oth, wi, wo, s, p, es):
    shape = e_own.shape
    return pl.pallas_call(
        functools.partial(backward_body, t),
        out_shape=(
            VMEM(shape, F32),
            jax.ShapeDtypeStruct(shape, BF16),
            VMEM(p.shape, BF16),
            jax.ShapeDtypeStruct(es.shape, BF16),
        ),
        in_specs=[IN_SMEM] + [IN_VMEM] * 6 + [IN_HBM],
        out_specs=[IN_VMEM] * 3 + [IN_HBM],
        scratch_shapes=[VMEM((2 * shape[0], shape[1]), F32), pltpu.SemaphoreType.DMA((2,))],
        input_output_aliases={6: 2, 7: 3},
        compiler_params=params(14),
        name=f"backward_t{t}",
    )(flags, e_own, e_oth, wi, wo, s, p, es)


def norm_back_body(t, flags, q0, q1, q2, q3, g, gain, n_save, r_save, gg_in, out, gg):
    width = q0.shape[1]

    @pl.when(flags[t] > 0)
    def _():
        q = (q0[...] + q1[...].astype(F32)) + (q2[...].astype(F32) + q3[...].astype(F32))
        n = n_save[...]
        r = r_save[:, 0:1]
        qn = q * n
        gg[0:1, :] = jnp.sum(qn, axis=0, keepdims=True)
        dot = jnp.sum(qn * gain[...], axis=1, keepdims=True) / width
        back = r * (q * gain[...] - n * dot)
        out[...] = (back + g[...].astype(F32)).astype(BF16)


def norm_back_call(t, flags, terms, g, gain, n_save, r_save, gg):
    return pl.pallas_call(
        functools.partial(norm_back_body, t),
        out_shape=(jax.ShapeDtypeStruct(g.shape, BF16), VMEM(gg.shape, F32)),
        in_specs=[IN_SMEM] + [IN_VMEM] * 9,
        out_specs=[IN_VMEM] * 2,
        input_output_aliases={9: 1},
        compiler_params=params(4),
        name=f"norm_back_t{t}",
    )(flags, *terms, g, gain, n_save, r_save, gg)


def grads_body(side, us, u_peer, es, e_peer, wi, wo, z, p, gin, gout):
    at = pl.multiple_of(pl.program_id(0) * TILE, TILE)
    cols = pl.ds(at, TILE)
    half = gin.shape[0]
    mine = pl.ds(pl.multiple_of(side[0] * half, half), half)
    a = jnp.dot(u_peer[...], wi[:, cols], preferred_element_type=F32)
    zf, slope = gelu_both(a)
    dz = lax.dot_general(e_peer[...], wo[cols, :], NT, preferred_element_type=F32)
    gi = lax.dot_general(us[:, mine], p[:, cols], TN, preferred_element_type=F32)
    gi += lax.dot_general(
        u_peer[:, mine], (dz * slope).astype(BF16), TN, preferred_element_type=F32
    )
    gin[...] = gi.astype(BF16)
    go = lax.dot_general(z[:, cols], es[:, mine], TN, preferred_element_type=F32)
    go += lax.dot_general(zf.astype(BF16), e_peer[:, mine], TN, preferred_element_type=F32)
    gout[...] = go.astype(BF16)


def grads_call(side, us, u_peer, es, e_peer, wi, wo, z, p):
    hidden = wi.shape[1]
    half = us.shape[1] // 2
    return pl.pallas_call(
        grads_body,
        grid=(hidden // TILE,),
        out_shape=(
            jax.ShapeDtypeStruct((half, hidden), BF16),
            jax.ShapeDtypeStruct((hidden, half), BF16),
        ),
        in_specs=[IN_SMEM] + [IN_VMEM] * 8,
        out_specs=[
            pl.BlockSpec((half, TILE), lambda j: (0, j)),
            pl.BlockSpec((TILE, half), lambda j: (j, 0)),
        ],
        compiler_params=params(20),
        name="weight_grads",
    )(side, us, u_peer, es, e_peer, wi, wo, z, p)


def shards(inputs, cotangent, gain, weight_in, weight_out):
    stages = lax.axis_size("pipe")
    ways = lax.axis_size("mp")
    stage = lax.axis_index("pipe")
    part = lax.axis_index("mp")
    replica = lax.axis_index("dp")
    core = lax.rem(part, 2)
    chip = part // 2
    micro, rows, width = inputs.shape
    full = gain.shape[1]
    hidden = weight_in.shape[2]
    ring = ways // 2
    all_rows = micro * rows
    chunk = all_rows // ways

    core_pairs = [(i, i ^ 1) for i in range(ways)]
    dp_pairs = [(0, 1), (1, 0)]

    def turned(i, turn):
        return ((i // 2 + turn) % ring) * 2 + i % 2

    def swap(block):
        return lax.ppermute(block, "mp", core_pairs)

    def spread(block, by):
        out = []
        for d in range(ring):
            pairs = [
                (k * ways + i, ((k + by) % stages) * ways + turned(i, d))
                for k in range(stages)
                for i in range(ways)
            ]
            out.append(lax.ppermute(block, ("pipe", "mp"), pairs))
        return out

    def collect(own, other):
        total = own + swap(other).astype(F32)
        terms = [total[:chunk]]
        for d in range(1, ring):
            slot = ring - d
            block = total[slot * chunk : (slot + 1) * chunk].astype(BF16)
            terms.append(lax.ppermute(block, "mp", [(i, turned(i, d)) for i in range(ways)]))
        return terms

    flags = (jnp.arange(stages, dtype=jnp.int32) == stage).astype(jnp.int32)

    both = jnp.stack([inputs, cotangent])
    both = lax.all_gather(both, "mp", axis=3, tiled=True).reshape(2, ways, chunk, full)

    def slots(array, side):
        places = [side * ring + lax.rem(chip - d + ring, ring) for d in range(ring)]
        return [lax.dynamic_index_in_dim(array, at, 0, keepdims=False) for at in places]

    x_first = slots(both[0], core)
    e_first = slots(both[1], core)
    e_second = slots(both[1], 1 - core)
    wi, wo = load_weights(weight_in[0], weight_out[0])
    z, s, p, n_save, r_save, gg = alloc(
        [(all_rows, hidden)] * 3 + [(chunk, full), (chunk, 128), (8, full)],
        [BF16, BF16, BF16, F32, F32, F32],
    )
    us = jnp.zeros((all_rows, full), BF16)
    es = jnp.zeros((all_rows, full), BF16)

    incoming = x_first
    for t in range(stages):
        last = t == stages - 1
        u_own, n_save, r_save = norm_call(t, flags, incoming, gain, n_save, r_save)
        u_oth = swap(u_own)
        p_own, p_oth, z, s, us = forward_call(t, last, flags, u_own, u_oth, wi, wo, z, s, us)
        if not last:
            t0, t1, t2, t3 = collect(p_own, p_oth)
            total = (t0 + t1.astype(F32)) + (t2.astype(F32) + t3.astype(F32))
            block = (incoming[0].astype(F32) + total).astype(BF16)
            incoming = spread(block, 1)

    u_peer = lax.ppermute(us, "dp", dp_pairs)

    incoming = e_first
    for t in range(stages - 1, -1, -1):
        e_own = jnp.concatenate(incoming, axis=0)
        e_oth = jnp.concatenate(e_second, axis=0) if t == stages - 1 else swap(e_own)
        q_own, q_oth, p, es = backward_call(t, flags, e_own, e_oth, wi, wo, s, p, es)
        if t == 0:
            e_peer = lax.ppermute(es, "dp", dp_pairs)
        block, gg = norm_back_call(
            t, flags, collect(q_own, q_oth), incoming[0], gain, n_save, r_save, gg
        )
        if t > 0:
            incoming = spread(block, -1)

    side = replica.astype(jnp.int32).reshape(1)
    grad_in, grad_out = grads_call(side, us, u_peer, es, e_peer, wi, wo, z, p)
    sums = gg
    sums = sums + lax.ppermute(sums, "dp", dp_pairs)
    sums = sums + swap(sums)
    sums = sums + lax.ppermute(sums, "mp", [(i, i ^ 2) for i in range(ways)])
    sums = sums + lax.ppermute(sums, "mp", [(i, i ^ 4) for i in range(ways)])
    grad_gain = lax.dynamic_slice_in_dim(sums[0:1], part * width, width, 1)
    return (grad_in[None], grad_out[None], grad_gain)


def solution(mesh):
    in_specs = (
        P(None, "dp", "mp"),
        P(None, "dp", "mp"),
        P("pipe", None),
        P("pipe", None, "mp"),
        P("pipe", "mp", None),
    )
    out_specs = (P("pipe", "dp", "mp"), P("pipe", "mp", "dp"), P("pipe", "mp"))
    return jax.shard_map(shards, mesh=mesh, in_specs=in_specs, out_specs=out_specs, check_vma=False)
```

```python
import functools
import math

import jax
import jax.numpy as jnp
from jax import lax
from jax.experimental import pallas as pl
from jax.experimental.pallas import tpu as pltpu
from jax.sharding import PartitionSpec as P

GELU_COEF = math.sqrt(2.0 / math.pi)
CUBIC_COEF = 0.044715
NORM_EPS = 1e-06
BF16 = jnp.bfloat16
F32 = jnp.float32
NT = (((1,), (1,)), ((), ()))
TN = (((0,), (0,)), ((), ()))
MIB = 2**20
FWD_TILE = 256
BWD_TILE = 1024
GRAD_TILE = 512
REPLICA, CORE, CHIP = 9, 10, 11
VMEM = pltpu.VMEM
IN_VMEM = pl.BlockSpec(memory_space=pltpu.VMEM)
IN_SMEM = pl.BlockSpec(memory_space=pltpu.SMEM)
ANYWHERE = pl.BlockSpec(memory_space=pl.ANY)
IN_HBM = pl.BlockSpec(memory_space=pltpu.HBM)


def params(mib):
    return pltpu.CompilerParams(vmem_limit_bytes=int(mib * MIB))


def gelu_both(a):
    a2 = a * a
    t = jnp.tanh(a * (GELU_COEF + (GELU_COEF * CUBIC_COEF) * a2))
    h = 0.5 + 0.5 * t
    z = a * h
    slope = h + (a * (0.5 - 0.5 * t * t)) * (GELU_COEF + (3.0 * GELU_COEF * CUBIC_COEF) * a2)
    return z, slope


def load_body(after, wi, wo, wi_out, wo_out, z, s, p, n_save, r_save, gg, sems):
    first = pltpu.make_async_copy(wi.at[0], wi_out, sems.at[0])
    second = pltpu.make_async_copy(wo.at[0], wo_out, sems.at[1])
    first.start()
    second.start()
    gg[...] = jnp.zeros_like(gg)
    first.wait()
    second.wait()


def load_weights(after, wi, wo, saves):
    return pl.pallas_call(
        load_body,
        out_shape=(VMEM(wi.shape[1:], wi.dtype), VMEM(wo.shape[1:], wo.dtype))
        + tuple(VMEM(shape, kind) for shape, kind in saves),
        in_specs=[ANYWHERE] + [IN_HBM] * 2,
        out_specs=[IN_VMEM] * (2 + len(saves)),
        scratch_shapes=[pltpu.SemaphoreType.DMA((2,))],
        compiler_params=params(38),
        name="load_weights",
    )(after, wi, wo)


def pick_body(ring, sides, info, parts, *outs):
    chunk, width = parts.shape[2], parts.shape[3]
    for side, out in zip(sides, outs):
        half = info[CORE] if side == 0 else 1 - info[CORE]
        for d in range(ring):
            at = half * ring + lax.rem(info[CHIP] - d + ring, ring)
            for k in range(parts.shape[0]):
                out[d * chunk : (d + 1) * chunk, k * width : (k + 1) * width] = parts[k, at]


def pick_call(info, parts, ring, sides, name):
    ways, _, chunk, width = parts.shape
    return pl.pallas_call(
        functools.partial(pick_body, ring, sides),
        out_shape=(jax.ShapeDtypeStruct((ring * chunk, ways * width), BF16),) * len(sides),
        in_specs=[IN_SMEM, IN_VMEM],
        out_specs=[IN_VMEM] * len(sides),
        compiler_params=params(4),
        name=name,
    )(info, parts)


def after_body(x, tie, out):
    out[...] = x[...]


def after_call(x, tie, name):
    return pl.pallas_call(
        after_body,
        out_shape=jax.ShapeDtypeStruct(x.shape, x.dtype),
        in_specs=[IN_VMEM, ANYWHERE],
        out_specs=IN_VMEM,
        compiler_params=params(1),
        name=name,
    )(x, tie)


def total_of(pieces):
    vals = [piece[...].astype(F32) for piece in pieces]
    while len(vals) > 1:
        vals = [a + b for a, b in zip(vals[::2], vals[1::2])]
    return vals[0]


def norm_body(t, count, ties, info, *refs):
    pieces, gain = refs[:count], refs[count]
    u_out, x_out, n_save, r_save = refs[count + 3 + ties :]
    chunk = x_out.shape[0]

    @pl.when(info[t] > 0)
    def _():
        for d in range(4):
            x = (pieces[d][...] if count == 4 else pieces[0][d * chunk : (d + 1) * chunk, :]).astype(F32)
            r = lax.rsqrt(jnp.mean(x * x, axis=1, keepdims=True) + NORM_EPS)
            n = x * r
            u_out[d * chunk : (d + 1) * chunk, :] = (n * gain[...]).astype(BF16)
            if d == 0:
                x_out[...] = x
                n_save[...] = n
                r_save[...] = jnp.broadcast_to(r, r_save.shape)


def norm_call(t, info, pieces, gain, n_save, r_save, ties):
    count = len(pieces)
    chunk, width = n_save.shape
    return pl.pallas_call(
        functools.partial(norm_body, t, count, len(ties)),
        out_shape=(
            jax.ShapeDtypeStruct((4 * chunk, width), BF16),
            VMEM((chunk, width), F32),
            VMEM(n_save.shape, F32),
            VMEM(r_save.shape, F32),
        ),
        in_specs=[IN_SMEM] + [IN_VMEM] * (count + 3) + [ANYWHERE] * len(ties),
        out_specs=[IN_VMEM] * 4,
        input_output_aliases={count + 2: 2, count + 3: 3},
        compiler_params=params(4),
        name=f"norm_t{t}",
    )(info, *pieces, gain, n_save, r_save, *ties)


def forward_body(t, side, last, info, u, wi, wo, z_in, s_in, out, z, s, acc):
    rows = u.shape[0]

    @pl.when(info[t] > 0)
    def _():
        here = slice(side * rows, (side + 1) * rows)
        for j in range(wi.shape[1] // FWD_TILE):
            cols = slice(j * FWD_TILE, (j + 1) * FWD_TILE)
            a = jnp.dot(u[...], wi[:, cols], preferred_element_type=F32)
            zf, slope = gelu_both(a)
            zb = zf.astype(BF16)
            z[here, cols] = zb
            s[here, cols] = slope.astype(BF16)
            if not last:
                d = jnp.dot(zb, wo[cols, :], preferred_element_type=F32)
                if j == 0:
                    acc[...] = d
                else:
                    acc[...] += d
        if not last:
            out[...] = acc[...].astype(out.dtype)


def forward_call(t, side, last, info, u, wi, wo, z, s):
    shape = u.shape
    return pl.pallas_call(
        functools.partial(forward_body, t, side, last),
        out_shape=(
            VMEM(shape, F32) if side == 0 else jax.ShapeDtypeStruct(shape, BF16),
            VMEM(z.shape, BF16),
            VMEM(s.shape, BF16),
        ),
        in_specs=[IN_SMEM] + [IN_VMEM] * 5,
        out_specs=[IN_VMEM] * 3,
        scratch_shapes=[VMEM(shape, F32)],
        input_output_aliases={4: 1, 5: 2},
        compiler_params=params(12),
        name=f"forward_t{t}_s{side}",
    )(info, u, wi, wo, z, s)


def backward_body(t, ties, info, e_own, e_oth, wi, wo, s, p_in, *refs):
    q_own, q_oth, p, acc = refs[ties:]
    half = e_own.shape[0]

    @pl.when(info[t] > 0)
    def _():
        e = jnp.concatenate([e_own[...], e_oth[...]], axis=0)
        for j in range(wi.shape[1] // BWD_TILE):
            cols = slice(j * BWD_TILE, (j + 1) * BWD_TILE)
            dz = lax.dot_general(e, wo[cols, :], NT, preferred_element_type=F32)
            pb = (dz * s[:, cols].astype(F32)).astype(BF16)
            p[:, cols] = pb
            d = lax.dot_general(pb, wi[:, cols], NT, preferred_element_type=F32)
            if j == 0:
                acc[...] = d
            else:
                acc[...] += d
        q_own[...] = acc[:half]
        q_oth[...] = acc[half:].astype(BF16)


def backward_call(t, info, e_own, e_oth, wi, wo, s, p, ties):
    shape = e_own.shape
    return pl.pallas_call(
        functools.partial(backward_body, t, len(ties)),
        out_shape=(VMEM(shape, F32), jax.ShapeDtypeStruct(shape, BF16), VMEM(p.shape, BF16)),
        in_specs=[IN_SMEM] + [IN_VMEM] * 6 + [ANYWHERE] * len(ties),
        out_specs=[IN_VMEM] * 3,
        scratch_shapes=[VMEM((2 * shape[0], shape[1]), F32)],
        input_output_aliases={6: 2},
        compiler_params=params(14),
        name=f"backward_t{t}",
    )(info, e_own, e_oth, wi, wo, s, p, *ties)


def norm_back_body(t, info, total, q1, q2, q3, g, gain, n_save, r_save, gg_in, *refs):
    out, gg = refs[-2:]
    chunk, width = out.shape

    @pl.when(info[t] > 0)
    def _():
        q = (total[:chunk, :] + q1[...].astype(F32)) + (q2[...].astype(F32) + q3[...].astype(F32))
        n = n_save[...]
        r = r_save[:, 0:1]
        qn = q * n
        gg[0:1, :] = jnp.sum(qn, axis=0, keepdims=True)
        dot = jnp.sum(qn * gain[...], axis=1, keepdims=True) / width
        back = r * (q * gain[...] - n * dot)
        out[...] = (back + g[:chunk, :].astype(F32)).astype(BF16)


def norm_back_call(t, info, terms, g, gain, n_save, r_save, gg, ties):
    return pl.pallas_call(
        functools.partial(norm_back_body, t),
        out_shape=(jax.ShapeDtypeStruct(n_save.shape, BF16), VMEM(gg.shape, F32)),
        in_specs=[IN_SMEM] + [IN_VMEM] * 9 + [ANYWHERE] * len(ties),
        out_specs=[IN_VMEM] * 2,
        input_output_aliases={9: 1},
        compiler_params=params(4),
        name=f"norm_back_t{t}",
    )(info, *terms, g, gain, n_save, r_save, gg, *ties)


def grads_body(groups, base, ties, info, *refs):
    us, up, es, ep = (refs[k * groups : (k + 1) * groups] for k in range(4))
    wi, wo, z, p = refs[4 * groups : 4 * groups + 4]
    gin, gout, *done = refs[4 * groups + 4 + ties :]
    if done:
        done[0][...] = jnp.zeros_like(done[0])
    tile = gin.shape[1]
    half = gin.shape[0]
    cols = pl.ds(pl.multiple_of((base + pl.program_id(0)) * tile, tile), tile)
    mine = pl.ds(pl.multiple_of(info[REPLICA] * half, half), half)

    def rows(parts, at):
        return jnp.concatenate([part[:, at] for part in parts], axis=0)

    every = slice(None)
    a = jnp.dot(rows(up, every), wi[:, cols], preferred_element_type=F32)
    zf, slope = gelu_both(a)
    dz = lax.dot_general(rows(ep, every), wo[cols, :], NT, preferred_element_type=F32)
    p_all = jnp.concatenate([p[:, cols], (dz * slope).astype(BF16)], axis=0)
    z_all = jnp.concatenate([z[:, cols], zf.astype(BF16)], axis=0)
    u_half = rows(us + up, mine)
    e_half = rows(es + ep, mine)
    gin[...] = lax.dot_general(u_half, p_all, TN, preferred_element_type=F32).astype(BF16)
    gout[...] = lax.dot_general(z_all, e_half, TN, preferred_element_type=F32).astype(BF16)


def grads_call(which, info, us, up, es, ep, wi, wo, z, p, ties):
    groups = len(us)
    hidden = wi.shape[1]
    half = us[0].shape[1] // 2
    steps = hidden // GRAD_TILE // 2
    base = which * steps
    return pl.pallas_call(
        functools.partial(grads_body, groups, base, len(ties)),
        grid=(steps,),
        out_shape=(
            jax.ShapeDtypeStruct((half, hidden), BF16),
            jax.ShapeDtypeStruct((hidden, half), BF16),
        )
        + (() if ties else (jax.ShapeDtypeStruct((8, 128), F32),)),
        in_specs=[IN_SMEM] + [IN_VMEM] * (4 * groups + 4) + [IN_HBM] * len(ties),
        out_specs=[
            pl.BlockSpec((half, GRAD_TILE), lambda j: (0, base + j)),
            pl.BlockSpec((GRAD_TILE, half), lambda j: (base + j, 0)),
        ]
        + ([] if ties else [IN_VMEM]),
        input_output_aliases={4 * groups + 5: 0, 4 * groups + 6: 1} if ties else {},
        compiler_params=params(14),
        cost_estimate=pl.CostEstimate(
            flops=2**33, bytes_accessed=2**23, transcendentals=0
        ),
        name=f"weight_grads_{which}",
    )(info, *us, *up, *es, *ep, wi, wo, z, p, *ties)


def quarters_body(ring, info, gg, *outs):
    width = outs[0].shape[1]
    for d in range(ring):
        at = lax.rem(info[CHIP] + d, ring) * width
        outs[d][...] = gg[:, pl.ds(pl.multiple_of(at, width), width)]


def quarters_call(info, gg, ring):
    width = gg.shape[1] // ring
    return pl.pallas_call(
        functools.partial(quarters_body, ring),
        out_shape=(jax.ShapeDtypeStruct((gg.shape[0], width), F32),) * ring,
        in_specs=[IN_SMEM, IN_VMEM],
        out_specs=[IN_VMEM] * ring,
        compiler_params=params(1),
        name="gain_quarters",
    )(info, gg)


def shares_body(count, info, *refs):
    kept, sent, total = refs[count], refs[count + 1], refs[count + 2]
    width = kept.shape[1]
    total[...] = total_of(refs[:count])
    core = info[CORE]
    kept[...] = total[:, pl.ds(pl.multiple_of(core * width, width), width)]
    sent[...] = total[:, pl.ds(pl.multiple_of((1 - core) * width, width), width)]


def shares_call(info, pieces):
    rows, width = pieces[0].shape
    return pl.pallas_call(
        functools.partial(shares_body, len(pieces)),
        out_shape=(jax.ShapeDtypeStruct((rows, width // 2), F32),) * 2,
        in_specs=[IN_SMEM] + [IN_VMEM] * len(pieces),
        out_specs=[IN_VMEM] * 2,
        scratch_shapes=[VMEM((rows, width), F32)],
        compiler_params=params(1),
        name="gain_shares",
    )(info, *pieces)


def pair_body(a, b, out):
    out[...] = a[...] + b[...]


def pair_call(a, b, name):
    return pl.pallas_call(
        pair_body,
        out_shape=jax.ShapeDtypeStruct(a.shape, F32),
        in_specs=[IN_VMEM] * 2,
        out_specs=IN_VMEM,
        compiler_params=params(1),
        name=name,
    )(a, b)


def shards(inputs, cotangent, gain, weight_in, weight_out):
    stages = lax.axis_size("pipe")
    ways = lax.axis_size("mp")
    stage = lax.axis_index("pipe")
    part = lax.axis_index("mp")
    replica = lax.axis_index("dp")
    micro, rows, width = inputs.shape
    full = gain.shape[1]
    hidden = weight_in.shape[2]
    ring = ways // 2
    all_rows = micro * rows
    chunk = all_rows // ways
    half = all_rows // 2

    core_pairs = [(i, i ^ 1) for i in range(ways)]
    dp_pairs = [(0, 1), (1, 0)]

    def turned(i, turn):
        return ((i // 2 + turn) % ring) * 2 + i % 2

    def swap(block):
        return lax.ppermute(block, "mp", core_pairs)

    def trade(block):
        return lax.ppermute(block, "dp", dp_pairs)

    def spread(block, by):
        out = []
        for d in range(ring):
            pairs = [
                (k * ways + i, ((k + by) % stages) * ways + turned(i, d))
                for k in range(stages)
                for i in range(ways)
            ]
            out.append(lax.ppermute(block, ("pipe", "mp"), pairs))
        return out

    def collect(own, other):
        total = own + swap(other).astype(F32)
        terms = [total]
        for d in range(1, ring):
            slot = ring - d
            block = total[slot * chunk : (slot + 1) * chunk].astype(BF16)
            terms.append(lax.ppermute(block, "mp", [(i, turned(i, d)) for i in range(ways)]))
        return terms

    place = jnp.arange(16, dtype=jnp.int32)
    info = (place == stage).astype(jnp.int32) * (place < stages).astype(jnp.int32)
    info = jnp.where(place == REPLICA, replica.astype(jnp.int32), info)
    info = jnp.where(place == CORE, (part & 1).astype(jnp.int32), info)
    info = jnp.where(place == CHIP, (part >> 1).astype(jnp.int32), info)

    def chosen(t, new, old):
        return jnp.where((info[t : t + 1] > 0)[:, None], new, old)

    def gathered(array):
        return lax.all_gather(array.reshape(ways, chunk, width), "mp", axis=0, tiled=False)

    (x_first,) = pick_call(info, gathered(inputs), ring, (0,), "pick_rows")
    wi, wo, z, s, p, n_save, r_save, gg = load_weights(
        x_first,
        weight_in,
        weight_out,
        [((all_rows, hidden), BF16)] * 3 + [((chunk, full), F32), ((chunk, 128), F32), ((8, full), F32)],
    )
    us = jnp.zeros((half, full), BF16)
    incoming = [x_first]
    ties = []
    for t in range(stages):
        last = t == stages - 1
        u_own, x_own, n_save, r_save = norm_call(t, info, incoming, gain, n_save, r_save, ties)
        u_oth = swap(u_own)
        p_own, z, s = forward_call(t, 0, last, info, u_own, wi, wo, z, s)
        p_oth, z, s = forward_call(t, 1, last, info, u_oth, wi, wo, z, s)
        us = chosen(t, u_own, us)
        if not last:
            t0, t1, t2, t3 = collect(p_own, p_oth)
            total = (t0[:chunk] + t1.astype(F32)) + (t2.astype(F32) + t3.astype(F32))
            block = (x_own + total).astype(BF16)
            incoming = spread(block, 1)
            ties = []
            if t == 1:
                late = after_call(cotangent, block, "hold_cotangent")
                e_first, e_second = pick_call(info, gathered(late), ring, (0, 1), "pick_cotangent")
                ties = [e_first]

    es = jnp.zeros((half, full), BF16)
    for t in range(stages - 1, -1, -1):
        if t == stages - 1:
            e_own, e_oth, g = e_first, e_second, e_first
        else:
            e_own, g = jnp.concatenate(incoming, axis=0), incoming[0]
            e_oth = swap(e_own)
        es = chosen(t, e_own, es)
        if t == 0:
            ep = trade(es)
        q_own, q_oth, p = backward_call(
            t, info, e_own, e_oth, wi, wo, s, p, us + up if t == stages - 2 else []
        )
        terms = collect(q_own, q_oth)
        ties = []
        if t == 0:
            es = [es, swap(es)]
            ep = [ep, swap(ep)]
            first = grads_call(0, info, us, up, es, ep, wi, wo, z, p, [])
            *first, done = first
            ties = [done]
        block, gg = norm_back_call(t, info, terms, g, gain, n_save, r_save, gg, ties)
        if t > 0:
            incoming = spread(block, -1)
        if t == stages - 1:
            us = after_call(us, block, "hold_rows")
            us = [us, swap(us)]
            up = trade(us[0])
            up = [up, swap(up)]

    mine, *theirs = quarters_call(info, gg, ring)
    shares = [mine] + [
        lax.ppermute(block, "mp", [(i, turned(i, d + 1)) for i in range(ways)])
        for d, block in enumerate(theirs)
    ]
    kept, sent = shares_call(info, shares)
    share = pair_call(kept, swap(sent), "gain_cores")
    grad_in, grad_out = grads_call(1, info, us, up, es, ep, wi, wo, z, p, list(first) + [share])
    grad_gain = pair_call(share, trade(share), "gain_replicas")[0:1]
    return (grad_in[None], grad_out[None], grad_gain)


def solution(mesh):
    in_specs = (
        P(None, "dp", "mp"),
        P(None, "dp", "mp"),
        P("pipe", None),
        P("pipe", None, "mp"),
        P("pipe", "mp", None),
    )
    out_specs = (P("pipe", "dp", "mp"), P("pipe", "mp", "dp"), P("pipe", "mp"))
    return jax.shard_map(shards, mesh=mesh, in_specs=in_specs, out_specs=out_specs, check_vma=False)
```

```python
import functools
import math

import jax
import jax.numpy as jnp
from jax import lax
from jax.experimental import pallas as pl
from jax.experimental.pallas import tpu as pltpu
from jax.sharding import PartitionSpec as P

GELU_COEF = math.sqrt(2.0 / math.pi)
CUBIC_COEF = 0.044715
NORM_EPS = 1e-06
BF16 = jnp.bfloat16
F32 = jnp.float32
NT = (((1,), (1,)), ((), ()))
TN = (((0,), (0,)), ((), ()))
MIB = 2**20
FWD_TILE = 256
BWD_TILE = 1024
GRAD_TILE = 512
REPLICA, CORE, CHIP = 9, 10, 11
VMEM = pltpu.VMEM
IN_VMEM = pl.BlockSpec(memory_space=pltpu.VMEM)
IN_SMEM = pl.BlockSpec(memory_space=pltpu.SMEM)
ANYWHERE = pl.BlockSpec(memory_space=pl.ANY)
IN_HBM = pl.BlockSpec(memory_space=pltpu.HBM)


def params(mib):
    return pltpu.CompilerParams(vmem_limit_bytes=int(mib * MIB))


def gelu_both(a):
    a2 = a * a
    t = jnp.tanh(a * (GELU_COEF + (GELU_COEF * CUBIC_COEF) * a2))
    h = 0.5 + 0.5 * t
    z = a * h
    slope = h + (a * (0.5 - 0.5 * t * t)) * (GELU_COEF + (3.0 * GELU_COEF * CUBIC_COEF) * a2)
    return z, slope


def load_body(after, wi, wo, wi_out, wo_out, z, s, p, n_save, r_save, gg, sems):
    first = pltpu.make_async_copy(wi.at[0], wi_out, sems.at[0])
    second = pltpu.make_async_copy(wo.at[0], wo_out, sems.at[1])
    first.start()
    second.start()
    gg[...] = jnp.zeros_like(gg)
    first.wait()
    second.wait()


def load_weights(after, wi, wo, saves):
    return pl.pallas_call(
        load_body,
        out_shape=(VMEM(wi.shape[1:], wi.dtype), VMEM(wo.shape[1:], wo.dtype))
        + tuple(VMEM(shape, kind) for shape, kind in saves),
        in_specs=[ANYWHERE] + [IN_HBM] * 2,
        out_specs=[IN_VMEM] * (2 + len(saves)),
        scratch_shapes=[pltpu.SemaphoreType.DMA((2,))],
        compiler_params=params(38),
        name="load_weights",
    )(after, wi, wo)


def pick_body(ring, sides, info, parts, *outs):
    chunk, width = parts.shape[2], parts.shape[3]
    for side, out in zip(sides, outs):
        half = info[CORE] if side == 0 else 1 - info[CORE]
        for d in range(ring):
            at = half * ring + lax.rem(info[CHIP] - d + ring, ring)
            for k in range(parts.shape[0]):
                out[d * chunk : (d + 1) * chunk, k * width : (k + 1) * width] = parts[k, at]


def pick_call(info, parts, ring, sides, name):
    ways, _, chunk, width = parts.shape
    return pl.pallas_call(
        functools.partial(pick_body, ring, sides),
        out_shape=(jax.ShapeDtypeStruct((ring * chunk, ways * width), BF16),) * len(sides),
        in_specs=[IN_SMEM, IN_VMEM],
        out_specs=[IN_VMEM] * len(sides),
        compiler_params=params(4),
        name=name,
    )(info, parts)


def after_body(x, tie, out):
    out[...] = x[...]


def after_call(x, tie, name):
    return pl.pallas_call(
        after_body,
        out_shape=jax.ShapeDtypeStruct(x.shape, x.dtype),
        in_specs=[IN_VMEM, ANYWHERE],
        out_specs=IN_VMEM,
        compiler_params=params(1),
        name=name,
    )(x, tie)


def total_of(pieces):
    vals = [piece[...].astype(F32) for piece in pieces]
    while len(vals) > 1:
        vals = [a + b for a, b in zip(vals[::2], vals[1::2])]
    return vals[0]


def norm_body(t, count, ties, info, *refs):
    pieces, gain = refs[:count], refs[count]
    u_out, x_out, n_save, r_save = refs[count + 3 + ties :]
    chunk = x_out.shape[0]

    @pl.when(info[t] > 0)
    def _():
        for d in range(4):
            x = (pieces[d][...] if count == 4 else pieces[0][d * chunk : (d + 1) * chunk, :]).astype(F32)
            r = lax.rsqrt(jnp.mean(x * x, axis=1, keepdims=True) + NORM_EPS)
            n = x * r
            u_out[d * chunk : (d + 1) * chunk, :] = (n * gain[...]).astype(BF16)
            if d == 0:
                x_out[...] = x
                n_save[...] = n
                r_save[...] = jnp.broadcast_to(r, r_save.shape)


def norm_call(t, info, pieces, gain, n_save, r_save, ties):
    count = len(pieces)
    chunk, width = n_save.shape
    return pl.pallas_call(
        functools.partial(norm_body, t, count, len(ties)),
        out_shape=(
            jax.ShapeDtypeStruct((4 * chunk, width), BF16),
            VMEM((chunk, width), F32),
            VMEM(n_save.shape, F32),
            VMEM(r_save.shape, F32),
        ),
        in_specs=[IN_SMEM] + [IN_VMEM] * (count + 3) + [ANYWHERE] * len(ties),
        out_specs=[IN_VMEM] * 4,
        input_output_aliases={count + 2: 2, count + 3: 3},
        compiler_params=params(4),
        name=f"norm_t{t}",
    )(info, *pieces, gain, n_save, r_save, *ties)


def forward_body(t, side, last, info, u, wi, wo, z_in, s_in, out, z, s, acc):
    rows = u.shape[0]

    @pl.when(info[t] > 0)
    def _():
        here = slice(side * rows, (side + 1) * rows)
        for j in range(wi.shape[1] // FWD_TILE):
            cols = slice(j * FWD_TILE, (j + 1) * FWD_TILE)
            a = jnp.dot(u[...], wi[:, cols], preferred_element_type=F32)
            zf, slope = gelu_both(a)
            zb = zf.astype(BF16)
            z[here, cols] = zb
            s[here, cols] = slope.astype(BF16)
            if not last:
                d = jnp.dot(zb, wo[cols, :], preferred_element_type=F32)
                if j == 0:
                    acc[...] = d
                else:
                    acc[...] += d
        if not last:
            out[...] = acc[...].astype(out.dtype)


def forward_call(t, side, last, info, u, wi, wo, z, s):
    shape = u.shape
    return pl.pallas_call(
        functools.partial(forward_body, t, side, last),
        out_shape=(
            VMEM(shape, F32) if side == 0 else jax.ShapeDtypeStruct(shape, BF16),
            VMEM(z.shape, BF16),
            VMEM(s.shape, BF16),
        ),
        in_specs=[IN_SMEM] + [IN_VMEM] * 5,
        out_specs=[IN_VMEM] * 3,
        scratch_shapes=[VMEM(shape, F32)],
        input_output_aliases={4: 1, 5: 2},
        compiler_params=params(12),
        name=f"forward_t{t}_s{side}",
    )(info, u, wi, wo, z, s)


def backward_body(t, ties, info, e_own, e_oth, wi, wo, s, p_in, *refs):
    q_own, q_oth, p, acc = refs[ties:]
    half = e_own.shape[0]

    @pl.when(info[t] > 0)
    def _():
        e = jnp.concatenate([e_own[...], e_oth[...]], axis=0)
        for j in range(wi.shape[1] // BWD_TILE):
            cols = slice(j * BWD_TILE, (j + 1) * BWD_TILE)
            dz = lax.dot_general(e, wo[cols, :], NT, preferred_element_type=F32)
            pb = (dz * s[:, cols].astype(F32)).astype(BF16)
            p[:, cols] = pb
            d = lax.dot_general(pb, wi[:, cols], NT, preferred_element_type=F32)
            if j == 0:
                acc[...] = d
            else:
                acc[...] += d
        q_own[...] = acc[:half]
        q_oth[...] = acc[half:].astype(BF16)


def backward_call(t, info, e_own, e_oth, wi, wo, s, p, ties):
    shape = e_own.shape
    return pl.pallas_call(
        functools.partial(backward_body, t, len(ties)),
        out_shape=(VMEM(shape, F32), jax.ShapeDtypeStruct(shape, BF16), VMEM(p.shape, BF16)),
        in_specs=[IN_SMEM] + [IN_VMEM] * 6 + [ANYWHERE] * len(ties),
        out_specs=[IN_VMEM] * 3,
        scratch_shapes=[VMEM((2 * shape[0], shape[1]), F32)],
        input_output_aliases={6: 2},
        compiler_params=params(14),
        name=f"backward_t{t}",
    )(info, e_own, e_oth, wi, wo, s, p, *ties)


def norm_back_body(t, info, total, q1, q2, q3, g, gain, n_save, r_save, gg_in, out, gg):
    chunk, width = out.shape

    @pl.when(info[t] > 0)
    def _():
        q = (total[:chunk, :] + q1[...].astype(F32)) + (q2[...].astype(F32) + q3[...].astype(F32))
        n = n_save[...]
        r = r_save[:, 0:1]
        qn = q * n
        gg[0:1, :] = jnp.sum(qn, axis=0, keepdims=True)
        dot = jnp.sum(qn * gain[...], axis=1, keepdims=True) / width
        back = r * (q * gain[...] - n * dot)
        out[...] = (back + g[:chunk, :].astype(F32)).astype(BF16)


def norm_back_call(t, info, terms, g, gain, n_save, r_save, gg):
    return pl.pallas_call(
        functools.partial(norm_back_body, t),
        out_shape=(jax.ShapeDtypeStruct(n_save.shape, BF16), VMEM(gg.shape, F32)),
        in_specs=[IN_SMEM] + [IN_VMEM] * 9,
        out_specs=[IN_VMEM] * 2,
        input_output_aliases={9: 1},
        compiler_params=params(4),
        name=f"norm_back_t{t}",
    )(info, *terms, g, gain, n_save, r_save, gg)


def gain_rows_body(t, info, q_own, q_oth, u_own, u_oth, gain, gg_in, gg):
    @pl.when(info[t] > 0)
    def _():
        own = jnp.sum(q_own[...] * u_own[...].astype(F32), axis=0, keepdims=True)
        other = jnp.sum(q_oth[...].astype(F32) * u_oth[...].astype(F32), axis=0, keepdims=True)
        gg[0:1, :] = (own + other) / gain[...]


def gain_rows_call(t, info, q_own, q_oth, u_own, u_oth, gain, gg):
    return pl.pallas_call(
        functools.partial(gain_rows_body, t),
        out_shape=VMEM(gg.shape, F32),
        in_specs=[IN_SMEM] + [IN_VMEM] * 6,
        out_specs=IN_VMEM,
        input_output_aliases={6: 0},
        compiler_params=params(4),
        name=f"gain_rows_t{t}",
    )(info, q_own, q_oth, u_own, u_oth, gain, gg)


def grads_body(groups, base, ties, info, *refs):
    us, up, es, ep = (refs[k * groups : (k + 1) * groups] for k in range(4))
    wi, wo, z, p = refs[4 * groups : 4 * groups + 4]
    gin, gout, *done = refs[4 * groups + 4 + ties :]
    if done:
        done[0][...] = jnp.zeros_like(done[0])
    tile = gin.shape[1]
    half = gin.shape[0]
    cols = pl.ds(pl.multiple_of((base + pl.program_id(0)) * tile, tile), tile)
    mine = pl.ds(pl.multiple_of(info[REPLICA] * half, half), half)

    def rows(parts, at):
        return jnp.concatenate([part[:, at] for part in parts], axis=0)

    every = slice(None)
    a = jnp.dot(rows(up, every), wi[:, cols], preferred_element_type=F32)
    zf, slope = gelu_both(a)
    dz = lax.dot_general(rows(ep, every), wo[cols, :], NT, preferred_element_type=F32)
    p_all = jnp.concatenate([p[:, cols], (dz * slope).astype(BF16)], axis=0)
    z_all = jnp.concatenate([z[:, cols], zf.astype(BF16)], axis=0)
    u_half = rows(us + up, mine)
    e_half = rows(es + ep, mine)
    gin[...] = lax.dot_general(u_half, p_all, TN, preferred_element_type=F32).astype(BF16)
    gout[...] = lax.dot_general(z_all, e_half, TN, preferred_element_type=F32).astype(BF16)


def grads_call(which, info, us, up, es, ep, wi, wo, z, p, ties):
    groups = len(us)
    hidden = wi.shape[1]
    half = us[0].shape[1] // 2
    steps = hidden // GRAD_TILE // 2
    base = which * steps
    return pl.pallas_call(
        functools.partial(grads_body, groups, base, len(ties)),
        grid=(steps,),
        out_shape=(
            jax.ShapeDtypeStruct((half, hidden), BF16),
            jax.ShapeDtypeStruct((hidden, half), BF16),
        )
        + (() if ties else (jax.ShapeDtypeStruct((8, 128), F32),)),
        in_specs=[IN_SMEM] + [IN_VMEM] * (4 * groups + 4) + [IN_HBM] * len(ties),
        out_specs=[
            pl.BlockSpec((half, GRAD_TILE), lambda j: (0, base + j)),
            pl.BlockSpec((GRAD_TILE, half), lambda j: (base + j, 0)),
        ]
        + ([] if ties else [IN_VMEM]),
        input_output_aliases={4 * groups + 5: 0, 4 * groups + 6: 1} if ties else {},
        compiler_params=params(14),
        cost_estimate=pl.CostEstimate(
            flops=2**33, bytes_accessed=2**23, transcendentals=0
        ),
        name=f"weight_grads_{which}",
    )(info, *us, *up, *es, *ep, wi, wo, z, p, *ties)


def quarters_body(ring, info, gg, *outs):
    width = outs[0].shape[1]
    for d in range(ring):
        at = lax.rem(info[CHIP] + d, ring) * width
        outs[d][...] = gg[:, pl.ds(pl.multiple_of(at, width), width)]


def quarters_call(info, gg, ring):
    width = gg.shape[1] // ring
    return pl.pallas_call(
        functools.partial(quarters_body, ring),
        out_shape=(jax.ShapeDtypeStruct((gg.shape[0], width), F32),) * ring,
        in_specs=[IN_SMEM, IN_VMEM],
        out_specs=[IN_VMEM] * ring,
        compiler_params=params(1),
        name="gain_quarters",
    )(info, gg)


def shares_body(count, info, *refs):
    kept, sent, total = refs[count + 1 :]
    width = kept.shape[1]
    total[...] = total_of(refs[:count])
    core = info[CORE]
    kept[...] = total[:, pl.ds(pl.multiple_of(core * width, width), width)]
    sent[...] = total[:, pl.ds(pl.multiple_of((1 - core) * width, width), width)]


def shares_call(info, pieces, after):
    rows, width = pieces[0].shape
    return pl.pallas_call(
        functools.partial(shares_body, len(pieces)),
        out_shape=(jax.ShapeDtypeStruct((rows, width // 2), F32),) * 2,
        in_specs=[IN_SMEM] + [IN_VMEM] * len(pieces) + [ANYWHERE],
        out_specs=[IN_VMEM] * 2,
        scratch_shapes=[VMEM((rows, width), F32)],
        compiler_params=params(1),
        name="gain_shares",
    )(info, *pieces, after)


def pair_body(a, b, out):
    out[...] = a[...] + b[...]


def pair_call(a, b, name):
    return pl.pallas_call(
        pair_body,
        out_shape=jax.ShapeDtypeStruct(a.shape, F32),
        in_specs=[IN_VMEM] * 2,
        out_specs=IN_VMEM,
        compiler_params=params(1),
        name=name,
    )(a, b)


def shards(inputs, cotangent, gain, weight_in, weight_out):
    stages = lax.axis_size("pipe")
    ways = lax.axis_size("mp")
    stage = lax.axis_index("pipe")
    part = lax.axis_index("mp")
    replica = lax.axis_index("dp")
    micro, rows, width = inputs.shape
    full = gain.shape[1]
    hidden = weight_in.shape[2]
    ring = ways // 2
    all_rows = micro * rows
    chunk = all_rows // ways
    half = all_rows // 2

    core_pairs = [(i, i ^ 1) for i in range(ways)]
    dp_pairs = [(0, 1), (1, 0)]

    def turned(i, turn):
        return ((i // 2 + turn) % ring) * 2 + i % 2

    def swap(block):
        return lax.ppermute(block, "mp", core_pairs)

    def trade(block):
        return lax.ppermute(block, "dp", dp_pairs)

    def spread(block, by):
        out = []
        for d in range(ring):
            pairs = [
                (k * ways + i, ((k + by) % stages) * ways + turned(i, d))
                for k in range(stages)
                for i in range(ways)
            ]
            out.append(lax.ppermute(block, ("pipe", "mp"), pairs))
        return out

    def collect(own, other):
        total = own + swap(other).astype(F32)
        terms = [total]
        for d in range(1, ring):
            slot = ring - d
            block = total[slot * chunk : (slot + 1) * chunk].astype(BF16)
            terms.append(lax.ppermute(block, "mp", [(i, turned(i, d)) for i in range(ways)]))
        return terms

    place = jnp.arange(16, dtype=jnp.int32)
    info = (place == stage).astype(jnp.int32) * (place < stages).astype(jnp.int32)
    info = jnp.where(place == REPLICA, replica.astype(jnp.int32), info)
    info = jnp.where(place == CORE, (part & 1).astype(jnp.int32), info)
    info = jnp.where(place == CHIP, (part >> 1).astype(jnp.int32), info)

    def chosen(t, new, old):
        return jnp.where((info[t : t + 1] > 0)[:, None], new, old)

    def gathered(array):
        return lax.all_gather(array.reshape(ways, chunk, width), "mp", axis=0, tiled=False)

    (x_first,) = pick_call(info, gathered(inputs), ring, (0,), "pick_rows")
    wi, wo, z, s, p, n_save, r_save, gg = load_weights(
        x_first,
        weight_in,
        weight_out,
        [((all_rows, hidden), BF16)] * 3 + [((chunk, full), F32), ((chunk, 128), F32), ((8, full), F32)],
    )
    us = jnp.zeros((half, full), BF16)
    incoming = [x_first]
    ties = []
    for t in range(stages):
        last = t == stages - 1
        u_own, x_own, n_save, r_save = norm_call(t, info, incoming, gain, n_save, r_save, ties)
        u_oth = swap(u_own)
        p_own, z, s = forward_call(t, 0, last, info, u_own, wi, wo, z, s)
        p_oth, z, s = forward_call(t, 1, last, info, u_oth, wi, wo, z, s)
        us = chosen(t, u_own, us)
        if not last:
            t0, t1, t2, t3 = collect(p_own, p_oth)
            total = (t0[:chunk] + t1.astype(F32)) + (t2.astype(F32) + t3.astype(F32))
            block = (x_own + total).astype(BF16)
            incoming = spread(block, 1)
            ties = []
            if t == 1:
                late = after_call(cotangent, block, "hold_cotangent")
                e_first, e_second = pick_call(info, gathered(late), ring, (0, 1), "pick_cotangent")
                ties = [e_first]

    es = jnp.zeros((half, full), BF16)
    for t in range(stages - 1, -1, -1):
        if t == stages - 1:
            e_own, e_oth, g = e_first, e_second, e_first
        else:
            e_own, g = jnp.concatenate(incoming, axis=0), incoming[0]
            e_oth = swap(e_own)
        es = chosen(t, e_own, es)
        if t == 0:
            ep = trade(es)
        q_own, q_oth, p = backward_call(
            t, info, e_own, e_oth, wi, wo, s, p, us + up if t == stages - 2 else []
        )
        if t > 0:
            terms = collect(q_own, q_oth)
            block, gg = norm_back_call(t, info, terms, g, gain, n_save, r_save, gg)
            incoming = spread(block, -1)
        else:
            gg = gain_rows_call(t, info, q_own, q_oth, *us, gain, gg)
        if t == stages - 1:
            us = after_call(us, block, "hold_rows")
            us = [us, swap(us)]
            up = trade(us[0])
            up = [up, swap(up)]

    es = [es, swap(es)]
    ep = after_call(ep, q_oth, "hold_peer")
    ep = [ep, swap(ep)]
    mine, *theirs = quarters_call(info, gg, ring)
    shares = [mine] + [
        lax.ppermute(block, "mp", [(i, turned(i, d + 1)) for i in range(ways)])
        for d, block in enumerate(theirs)
    ]
    *first, done = grads_call(0, info, us, up, es, ep, wi, wo, z, p, [])
    kept, sent = shares_call(info, shares, done)
    share = pair_call(kept, swap(sent), "gain_cores")
    grad_in, grad_out = grads_call(1, info, us, up, es, ep, wi, wo, z, p, list(first) + [share])
    grad_gain = pair_call(share, trade(share), "gain_replicas")[0:1]
    return (grad_in[None], grad_out[None], grad_gain)


def solution(mesh):
    in_specs = (
        P(None, "dp", "mp"),
        P(None, "dp", "mp"),
        P("pipe", None),
        P("pipe", None, "mp"),
        P("pipe", "mp", None),
    )
    out_specs = (P("pipe", "dp", "mp"), P("pipe", "mp", "dp"), P("pipe", "mp"))
    return jax.shard_map(shards, mesh=mesh, in_specs=in_specs, out_specs=out_specs, check_vma=False)
```
